32 devices in a mesh: parts: 2 (over x), rows: 8 (over z, y), aux: 2 (over core).
Axes of the slice: x: 2, y: 2, z: 4, core: 2. Of those that a mesh axis runs over, the one named last changes fastest.
Arguments:
- integrals: bfloat16 [4, 2048, 2048], P(('parts', 'aux'), 'rows'), parts along dimension 0, may hold values from -6 to 6
- coefficients: bfloat16 [4096, 256], P(('parts', 'rows')), parts along dimension 0, may hold values from -0.046875 to 0.046875
- screen: int32 [4, 8, 8], P(('parts', 'aux'), 'rows'), parts along dimension 0, may hold values 0 or 1
Outputs:
- exchange: bfloat16 [4096, 2048], P(('parts', 'rows'), 'aux'), parts along dimension 0
The draws below stay inside these ranges and needn't reach their ends.
There are 2 independent parts, one for each index of `parts`. The reference program is written for one: setup_inputs(seed, part) draws one part's arguments, and reference() takes and returns one part's arrays. A program takes and returns all parts, laid end to end along the dimension named above; each array names one. Nothing has to cross between parts.
All inputs are finite; a program needn't handle non-finite values. No bound on the sum of `screen` on one device may be relied on, other than what follows from the above.
Results may differ from the reference program's by a relative error of at most 0.0061.
Values may be sent and summed in bfloat16 or wider, within the bound.
A program may use at most 128 MiB of HBM per device.

```python
import jax
import jax.numpy as jnp
from jax import lax

NOCC = 256
BF_DEV = 256
AUX_DEV = 1
NBF = 2048
NBLK = 8
NAUX = 2
N_AUX = 2


def plant(entries, key, least, high):
    longest = entries.shape.index(max(entries.shape))
    spots = []
    for shift in (0, 1):
        where = [jax.random.randint(jax.random.fold_in(key, axis), (), 0, length) for axis, length in enumerate(entries.shape)]
        where[longest] = (where[longest] + shift) % entries.shape[longest]
        spots.append(tuple(where))
    return entries.at[spots[0]].set(least).at[spots[1]].set(high)


def level_of(key, shape, cuts, low, largest):
    level = 1.0
    for position, parts in cuts:
        draws = jax.random.uniform(jax.random.fold_in(jax.random.fold_in(key, 6), position), (parts,), jnp.float32, low / len(cuts), largest / len(cuts))
        level = level * jnp.repeat(jnp.exp(draws), shape[position] // parts).reshape((-1,) + (1,) * (len(shape) - 1 - position))
    return level


def gaussian(own_key, dims, width, reach, split=(), kind=jnp.bfloat16):
    values = jax.random.normal(own_key, dims, jnp.float32) * width
    if len(split) > 0:
        values = level_of(own_key, dims, split, -0.22, 0.18) * values
    return jnp.clip(values, min=-reach, max=reach).astype(kind)


def setup_inputs(seed: int = 0, part: int = 0) -> dict:
    key_list = jax.random.split(jax.random.key(seed), 4)
    part_keys = jax.random.split(jax.random.fold_in(key_list[3], part), 4)
    return {
        "integrals": gaussian(part_keys[0], (NAUX, NBF, NBF), 1.0, 6.0, ((0, 2), (1, 8))),
        "coefficients": gaussian(part_keys[1], (NBF, NOCC), (8 * NBF) ** -0.5, 0.046875, ((0, 8),)),
        "screen": plant((jax.random.randint(part_keys[2], (N_AUX, NBLK, NBLK), 0, 3) < 2).astype(jnp.int32), jax.random.fold_in(part_keys[2], 1), 0, 1),
    }


def reference(integrals, coefficients, screen):
    def half_block(index):
        start = (index * BF_DEV).astype(jnp.int32)
        rows_part = lax.dynamic_slice_in_dim(integrals, start, BF_DEV, 1)
        tiles = lax.dynamic_index_in_dim(screen, index, 1, keepdims=False)
        flags = jnp.repeat(jnp.repeat(tiles, AUX_DEV, axis=0), BF_DEV, axis=1).astype(jnp.bfloat16)
        masked = rows_part * flags[:, None, :]
        out = jnp.dot(masked.reshape(NAUX * BF_DEV, NBF), coefficients, preferred_element_type=jnp.float32)
        return out.reshape(NAUX, BF_DEV, NOCC).astype(jnp.bfloat16)

    half = lax.map(half_block, jnp.arange(NBLK, dtype=jnp.int32))
    half = jnp.transpose(half, (1, 0, 2, 3)).reshape(N_AUX, AUX_DEV, NBF, NOCC)
    grouped = jnp.transpose(half, (0, 2, 1, 3)).reshape(N_AUX, NBF, AUX_DEV * NOCC)

    def exchange_block(index):
        start = (index * BF_DEV).astype(jnp.int32)
        total = jnp.zeros((BF_DEV, NBF), jnp.float32)
        for group in range(N_AUX):
            left = lax.dynamic_slice_in_dim(grouped[group], start, BF_DEV, 0)
            partial_rows = jnp.dot(left, grouped[group].T, preferred_element_type=jnp.float32).astype(jnp.bfloat16)
            partial_rows = lax.optimization_barrier(partial_rows)
            total = total + partial_rows.astype(jnp.float32)
        return total.astype(jnp.bfloat16)

    blocks = lax.map(exchange_block, jnp.arange(NBLK, dtype=jnp.int32))
    return blocks.reshape(NBF, NBF)
```

```python
import functools

import jax
import jax.numpy as jnp
from jax import lax
from jax.experimental import pallas as pl
from jax.experimental.pallas import tpu as pltpu
from jax.sharding import PartitionSpec as P

MESH = pl.DeviceIdType.MESH


def split_rows(n):
    inner = 1
    while inner * inner * 4 <= n:
        inner *= 2
    return n // inner, inner


def table(outer, rank, z):
    code = 0
    for place in range(outer):
        others = sorted((k for k in range(outer) if k != place), key=lambda k: (abs(k - place), k))
        code += others[rank] * outer**place
    power = 1
    bit = 1
    while bit < outer:
        power = power * (1 + (outer**bit - 1) * ((z // bit) % 2))
        bit *= 2
    return (code // power) % outer


def remote(src, dst, send, recv, rows, aux):
    return pltpu.make_async_remote_copy(
        src_ref=src,
        dst_ref=dst,
        send_sem=send,
        recv_sem=recv,
        device_id={"rows": rows, "aux": aux},
        device_id_type=MESH,
    )


def kernel(
    outer,
    inner,
    a_hbm,
    c_hbm,
    screen,
    out_hbm,
    a,
    c,
    acc,
    left,
    h,
    out,
    load_sem,
    store_sem,
    cz_send,
    cz_recv,
    cy_send,
    cy_recv,
    cs_send,
    cs_recv,
    hs_send,
    hs_recv,
    hz_send,
    hz_recv,
    hy_send,
    hf_send,
    hy_recv,
):
    n = outer * inner
    block = c_hbm.shape[0]
    part = block // 2
    ho = outer // 2
    me = lax.axis_index("rows")
    core = lax.axis_index("aux")
    sib = 1 - core
    z = me // inner
    y = me % inner
    owner = z // ho

    load_a = pltpu.make_async_copy(a_hbm.at[0], a, load_sem.at[0])
    load_c = pltpu.make_async_copy(c_hbm, c.at[me], load_sem.at[1])
    load_c.start()
    load_a.start()

    zs = [table(outer, rank, z) for rank in range(outer - 1)]
    ys = [(y + k) % inner for k in range(1, inner)]

    barrier = pltpu.get_barrier_semaphore()
    for k in range(2):
        for other in zs:
            pl.semaphore_signal(
                barrier, inc=1, device_id={"rows": other * inner + y, "aux": k}, device_id_type=MESH
            )
        for other in ys:
            pl.semaphore_signal(
                barrier, inc=1, device_id={"rows": z * inner + other, "aux": k}, device_id_type=MESH
            )
    pl.semaphore_signal(barrier, inc=1, device_id={"rows": me, "aux": sib}, device_id_type=MESH)
    pl.semaphore_wait(barrier, 2 * (outer - 1) + 2 * (inner - 1) + 1)

    def piece(s, half):
        return c.at[s, pl.ds(pl.multiple_of(half * part, part), part)]

    sends = []

    def c_along_z(other):
        own = piece(me, core)
        copy = remote(own, own, cz_send.at[other], cz_recv.at[z], other * inner + y, core)
        copy.start()
        sends.append(copy)

    def c_along_y(source):
        block_at = piece(source * inner + y, core)
        for other in ys:
            copy = remote(
                block_at,
                block_at,
                cy_send.at[source, other],
                cy_recv.at[source, y],
                z * inner + other,
                core,
            )
            copy.start()
            sends.append(copy)

    def c_to_sibling(s):
        block_at = piece(s, core)
        copy = remote(block_at, block_at, cs_send.at[s], cs_recv.at[s], me, sib)
        copy.start()
        sends.append(copy)

    def wait_recv(ref, sem):
        remote(ref, ref, cz_send.at[0], sem, me, sib).wait_recv()

    load_c.wait()
    c_along_y(z)
    for other in zs:
        c_along_z(other)
    load_a.wait()

    def product(s):
        columns = pl.ds(pl.multiple_of(s * block, block), block)
        flag = screen[0, 0, s].astype(jnp.float32)
        return flag * jnp.dot(a[:, columns], c[s], preferred_element_type=jnp.float32)

    acc[...] = product(me)

    for source in zs:
        wait_recv(piece(source * inner + y, core), cz_recv.at[source])
        c_along_y(source)
        c_to_sibling(source * inner + y)
    for source in zs:
        s = source * inner + y
        wait_recv(piece(s, sib), cs_recv.at[s])
        acc[...] += product(s)
    arrivals = [(source, other) for source in [z] + zs for other in ys]
    for source, other in arrivals:
        s = source * inner + other
        wait_recv(piece(s, core), cy_recv.at[source, other])
        c_to_sibling(s)
    for source, other in arrivals:
        s = source * inner + other
        wait_recv(piece(s, sib), cs_recv.at[s])
        acc[...] += product(s)

    left[core] = acc[...].astype(left.dtype)

    mine = left.at[core]

    def slot(aux, source, yy):
        return h.at[aux, (source % ho) * inner + yy]

    for other in ys:
        copy = remote(
            mine, slot(core, z, y), hy_send.at[other], hy_recv.at[core, z, y], z * inner + other, owner
        )
        copy.start()
        sends.append(copy)
    for other in zs:
        copy = remote(
            mine, slot(core, z, y), hz_send.at[other], hz_recv.at[core, z], other * inner + y, owner
        )
        copy.start()
        sends.append(copy)
    to_sib = remote(mine, mine, hs_send.at[0], hs_recv.at[0], me, sib)
    to_sib.start()
    sends.append(to_sib)

    def forward(aux, source, other):
        ref = slot(aux, source, y)
        return remote(
            ref, ref, hf_send.at[aux, source, other], hy_recv.at[aux, source, y], z * inner + other, core
        )

    def emit(source, yy, right0, right1):
        at = (source % ho) * inner + yy
        nt = (((1,), (1,)), ((), ()))
        p0 = lax.dot_general(left[0], right0, nt, preferred_element_type=jnp.float32)
        p1 = lax.dot_general(left[1], right1, nt, preferred_element_type=jnp.float32)
        total = p0.astype(out.dtype).astype(jnp.float32) + p1.astype(out.dtype).astype(jnp.float32)
        columns = pl.ds(pl.multiple_of(at * block, block), block)
        out[:, columns] = total.astype(out.dtype)
        pltpu.make_async_copy(out.at[:, columns], out_hbm.at[:, columns], store_sem.at[at]).start()

    order = [core * ho + j + owner * (1 - core) * (ho - 1 - 2 * j) for j in range(ho)]

    for source in order:

        @pl.when(source != z)
        def _(source=source):
            for aux in range(2):
                wait_recv(slot(aux, source, y), hz_recv.at[aux, source])
                for other in ys:
                    forward(aux, source, other).start()

    wait_recv(left.at[sib], hs_recv.at[0])

    @pl.when(owner == core)
    def _():
        emit(z, y, left[0], left[1])

    for source in order:

        @pl.when(source != z)
        def _(source=source):
            at = (source % ho) * inner + y
            emit(source, y, h[0, at], h[1, at])

    for source in order:
        for other in ys:
            for aux in range(2):
                wait_recv(slot(aux, source, other), hy_recv.at[aux, source, other])
            at = (source % ho) * inner + other
            emit(source, other, h[0, at], h[1, at])

    for copy in sends:
        copy.wait_send()
    for source in order:

        @pl.when(source != z)
        def _(source=source):
            for aux in range(2):
                for other in ys:
                    forward(aux, source, other).wait_send()

    for at in range(n // 2):
        columns = pl.ds(at * block, block)
        pltpu.make_async_copy(out.at[:, columns], out_hbm.at[:, columns], store_sem.at[at]).wait()


def local(n, integrals, coefficients, screen):
    outer, inner = split_rows(n)
    block, occupied = coefficients.shape
    dma = pltpu.SemaphoreType.DMA
    basis = n * block
    return pl.pallas_call(
        functools.partial(kernel, outer, inner),
        out_shape=jax.ShapeDtypeStruct((block, basis // 2), jnp.bfloat16),
        in_specs=[
            pl.BlockSpec(memory_space=pl.ANY),
            pl.BlockSpec(memory_space=pl.ANY),
            pl.BlockSpec(memory_space=pltpu.SMEM),
        ],
        out_specs=pl.BlockSpec(memory_space=pl.ANY),
        scratch_shapes=[
            pltpu.VMEM((block, basis), jnp.bfloat16),
            pltpu.VMEM((n, block, occupied), jnp.bfloat16),
            pltpu.VMEM((block, occupied), jnp.float32),
            pltpu.VMEM((2, block, occupied), jnp.bfloat16),
            pltpu.VMEM((2, n // 2, block, occupied), jnp.bfloat16),
            pltpu.VMEM((block, basis // 2), jnp.bfloat16),
            dma((2,)),
            dma((n // 2,)),
            dma((outer,)),
            dma((outer,)),
            dma((outer, inner)),
            dma((outer, inner)),
            dma((n,)),
            dma((n,)),
            dma((1,)),
            dma((1,)),
            dma((outer,)),
            dma((2, outer)),
            dma((inner,)),
            dma((2, outer, inner)),
            dma((2, outer, inner)),
        ],
        compiler_params=pltpu.CompilerParams(
            collective_id=0, has_side_effects=True, vmem_limit_bytes=44 * 1024 * 1024
        ),
        cost_estimate=pl.CostEstimate(
            flops=4 * block * basis * occupied, bytes_accessed=4 * block * basis, transcendentals=0
        ),
    )(integrals, coefficients, screen)


def solution(mesh):
    in_specs = (
        P(("parts", "aux"), "rows", None),
        P(("parts", "rows"), None),
        P(("parts", "aux"), "rows", None),
    )
    out_specs = P(("parts", "rows"), "aux")
    body = functools.partial(local, mesh.shape["rows"])
    return jax.shard_map(body, mesh=mesh, in_specs=in_specs, out_specs=out_specs, check_vma=False)
```

```python
import functools

import jax
import jax.numpy as jnp
from jax import lax
from jax.experimental import pallas as pl
from jax.experimental.pallas import tpu as pltpu
from jax.sharding import PartitionSpec as P

MESH = pl.DeviceIdType.MESH
CHUNKS = 2


def split_rows(n):
    inner = 1
    while inner * inner * 4 <= n:
        inner *= 2
    return n // inner, inner


def table(outer, rank, z):
    code = 0
    for place in range(outer):
        others = sorted((k for k in range(outer) if k != place), key=lambda k: (abs(k - place), k))
        code += others[rank] * outer**place
    power = 1
    bit = 1
    while bit < outer:
        power = power * (1 + (outer**bit - 1) * ((z // bit) % 2))
        bit *= 2
    return (code // power) % outer


def remote(src, dst, send, recv, rows, aux):
    return pltpu.make_async_remote_copy(
        src_ref=src,
        dst_ref=dst,
        send_sem=send,
        recv_sem=recv,
        device_id={"rows": rows, "aux": aux},
        device_id_type=MESH,
    )


def kernel(
    outer,
    inner,
    a_hbm,
    c_hbm,
    screen_hbm,
    out_hbm,
    a,
    screen,
    c_own,
    ct,
    acc,
    own,
    left,
    h,
    out,
    load_sem,
    store_sem,
    a_send,
    a_recv,
    cz_send,
    cz_recv,
    cy_send,
    cy_recv,
    hs_send,
    hs_recv,
    hz_send,
    hz_recv,
    hy_send,
    hf_send,
    hy_recv,
    cf_send,
    ho_send,
):
    n = outer * inner
    block, occupied = c_hbm.shape
    ho = outer // 2
    width = occupied // 2
    ic = width // CHUNKS
    groups = 2 * CHUNKS
    me = lax.axis_index("rows")
    core = lax.axis_index("aux")
    sib = 1 - core
    z = me // inner
    y = me % inner
    owner = z // ho

    mine_i = pl.ds(pl.multiple_of(core * width, width), width)
    load_c = pltpu.make_async_copy(c_hbm.at[:, mine_i], c_own, load_sem.at[1])
    load_a = pltpu.make_async_copy(a_hbm.at[0], a.at[core], load_sem.at[0])
    load_s = pltpu.make_async_copy(screen_hbm, screen, load_sem.at[2])
    load_c.start()
    load_s.start()
    load_a.start()

    zs = [table(outer, rank, z) for rank in range(outer - 1)]
    ys = [(y + k) % inner for k in range(1, inner)]
    hub = outer == 4
    mate = z + 1 - 2 * (z % 2)
    inside = ((z + 1) // 2) % 2
    direct = [2 - z // 2, mate] if hub else zs[::-1]

    barrier = pltpu.get_barrier_semaphore()
    for k in range(2):
        for other in zs:
            pl.semaphore_signal(
                barrier, inc=1, device_id={"rows": other * inner + y, "aux": k}, device_id_type=MESH
            )
        for other in ys:
            pl.semaphore_signal(
                barrier, inc=1, device_id={"rows": z * inner + other, "aux": k}, device_id_type=MESH
            )
    pl.semaphore_signal(barrier, inc=1, device_id={"rows": me, "aux": sib}, device_id_type=MESH)

    load_c.wait()
    turned = c_own[...].T
    for q in range(CHUNKS):
        ct[q, me] = turned[q * ic : (q + 1) * ic]

    pl.semaphore_wait(barrier, 2 * (outer - 1) + 2 * (inner - 1) + 1)

    sends = []

    def start(copy):
        copy.start()
        sends.append(copy)

    def wait_recv(ref, sem):
        remote(ref, ref, a_send.at[0], sem, me, sib).wait_recv()

    def c_along_y(q, source):
        ref = ct.at[q, source * inner + y]
        for other in ys:
            start(
                remote(
                    ref,
                    ref,
                    cy_send.at[q, source, other],
                    cy_recv.at[q, source, y],
                    z * inner + other,
                    core,
                )
            )

    for q in range(CHUNKS):
        for other in direct:
            ref = ct.at[q, me]
            start(remote(ref, ref, cz_send.at[q, other], cz_recv.at[q, z], other * inner + y, core))
        c_along_y(q, z)

    load_s.wait()
    load_a.wait()
    for s in range(n):
        columns = pl.ds(s * block, block)
        flag = screen[0, 0, s].astype(jnp.float32)
        a[core, :, columns] = (a[core, :, columns].astype(jnp.float32) * flag).astype(a.dtype)
    start(remote(a.at[core], a.at[core], a_send.at[0], a_recv.at[0], me, sib))

    def c_onward(q, source):
        ref = ct.at[q, source * inner + y]
        return remote(
            ref, ref, cf_send.at[q, source], cz_recv.at[q, source], mate * inner + y, core
        )

    def c_from_z(q):
        for source in zs:
            wait_recv(ct.at[q, source * inner + y], cz_recv.at[q, source])
            if hub:

                @pl.when((inside == 1) & (source != mate))
                def _(source=source):
                    c_onward(q, source).start()

            c_along_y(q, source)

    nt = (((1,), (1,)), ((), ()))

    def product(q, s, first=False):
        columns = pl.ds(pl.multiple_of(s * block, block), block)
        for aux in range(2):
            term = lax.dot_general(
                ct[q, s], a[aux, :, columns], nt, preferred_element_type=jnp.float32
            )
            if first:
                acc[q, aux] = term
            else:
                acc[q, aux] += term

    def slot(source, yy):
        return (source % ho) * inner + yy

    def finish(q):
        for aux in range(2):
            own[core * CHUNKS + q, aux] = acc[q, aux].astype(own.dtype)
        g = core * CHUNKS + q
        ref = own.at[g]
        dst = h.at[slot(z, y), g]
        for other in direct:
            start(remote(ref, dst, hz_send.at[q, other], hz_recv.at[g, z], other * inner + y, owner))
        for other in ys:
            start(
                remote(ref, dst, hy_send.at[q, other], hy_recv.at[g, z, y], z * inner + other, owner)
            )
        start(remote(ref, ref, hs_send.at[q], hs_recv.at[q], me, sib))

    c_from_z(0)
    wait_recv(a.at[sib], a_recv.at[0])
    product(0, me, True)
    for source in zs:
        product(0, source * inner + y)
    for q in range(CHUNKS):
        if q + 1 < CHUNKS:
            c_from_z(q + 1)
        for source in [z] + zs:
            for other in ys:
                s = source * inner + other
                wait_recv(ct.at[q, s], cy_recv.at[q, source, other])
                product(q, s)
        finish(q)
        if q + 1 < CHUNKS:
            product(q + 1, me, True)
            for source in zs:
                product(q + 1, source * inner + y)

    def forward(g, source, other):
        ref = h.at[slot(source, y), g]
        return remote(
            ref, ref, hf_send.at[g, source, other], hy_recv.at[g, source, y], z * inner + other, core
        )

    def onward(g, source):
        ref = h.at[slot(source, y), g]
        return remote(
            ref, ref, ho_send.at[g, source], hz_recv.at[g, source], mate * inner + y, core
        )

    order = [core * ho + j + owner * (1 - core) * (ho - 1 - 2 * j) for j in range(ho)]

    for q in range(CHUNKS):
        for source in order:

            @pl.when(source != z)
            def _(source=source, q=q):
                for k in range(2):
                    g = k * CHUNKS + q
                    wait_recv(h.at[slot(source, y), g], hz_recv.at[g, source])
                    if hub:

                        @pl.when((inside == 1) & (source != mate))
                        def _(source=source, g=g):
                            onward(g, source).start()

                    for other in ys:
                        forward(g, source, other).start()

    for q in range(CHUNKS):
        wait_recv(own.at[sib * CHUNKS + q], hs_recv.at[q])
    for aux in range(2):
        left[aux] = jnp.concatenate([own[g, aux] for g in range(groups)], axis=0).T

    def emit(at, right):
        total = 0.0
        for aux in range(2):
            whole = jnp.concatenate([right(g, aux) for g in range(groups)], axis=0)
            term = jnp.dot(left[aux], whole, preferred_element_type=jnp.float32)
            total = total + term.astype(out.dtype).astype(jnp.float32)
        columns = pl.ds(pl.multiple_of(at * block, block), block)
        out[:, columns] = total.astype(out.dtype)
        pltpu.make_async_copy(out.at[:, columns], out_hbm.at[:, columns], store_sem.at[at]).start()

    @pl.when(owner == core)
    def _():
        emit(slot(z, y), lambda g, aux: own[g, aux])

    for source in order:

        @pl.when(source != z)
        def _(source=source):
            at = slot(source, y)
            emit(at, lambda g, aux: h[at, g, aux])

    last = [core * ho + j + owner * (1 - core) * (ho - 1 - 2 * j) for j in range(ho)]
    for source in last:
        for other in ys:
            at = slot(source, other)
            for g in range(groups):
                wait_recv(h.at[at, g], hy_recv.at[g, source, other])
            emit(at, lambda g, aux, at=at: h[at, g, aux])

    for copy in sends:
        copy.wait_send()
    if hub:
        for source in zs:

            @pl.when((inside == 1) & (source != mate))
            def _(source=source):
                for q in range(CHUNKS):
                    c_onward(q, source).wait_send()

    for source in order:

        @pl.when(source != z)
        def _(source=source):
            for g in range(groups):
                for other in ys:
                    forward(g, source, other).wait_send()
                if hub:

                    @pl.when((inside == 1) & (source != mate))
                    def _(source=source, g=g):
                        onward(g, source).wait_send()


    for at in range(n // 2):
        columns = pl.ds(at * block, block)
        pltpu.make_async_copy(out.at[:, columns], out_hbm.at[:, columns], store_sem.at[at]).wait()


def local(n, integrals, coefficients, screen):
    outer, inner = split_rows(n)
    block, occupied = coefficients.shape
    dma = pltpu.SemaphoreType.DMA
    basis = n * block
    groups = 2 * CHUNKS
    ic = occupied // groups
    return pl.pallas_call(
        functools.partial(kernel, outer, inner),
        out_shape=jax.ShapeDtypeStruct((block, basis // 2), jnp.bfloat16),
        in_specs=[pl.BlockSpec(memory_space=pltpu.HBM)] * 3,
        out_specs=pl.BlockSpec(memory_space=pl.ANY),
        scratch_shapes=[
            pltpu.VMEM((2, block, basis), jnp.bfloat16),
            pltpu.SMEM(screen.shape, jnp.int32),
            pltpu.VMEM((block, occupied // 2), jnp.bfloat16),
            pltpu.VMEM((CHUNKS, n, ic, block), jnp.bfloat16),
            pltpu.VMEM((CHUNKS, 2, ic, block), jnp.float32),
            pltpu.VMEM((groups, 2, ic, block), jnp.bfloat16),
            pltpu.VMEM((2, block, occupied), jnp.bfloat16),
            pltpu.VMEM((n // 2, groups, 2, ic, block), jnp.bfloat16),
            pltpu.VMEM((block, basis // 2), jnp.bfloat16),
            dma((3,)),
            dma((n // 2,)),
            dma((1,)),
            dma((1,)),
            dma((CHUNKS, outer)),
            dma((CHUNKS, outer)),
            dma((CHUNKS, outer, inner)),
            dma((CHUNKS, outer, inner)),
            dma((CHUNKS,)),
            dma((CHUNKS,)),
            dma((CHUNKS, outer)),
            dma((groups, outer)),
            dma((CHUNKS, inner)),
            dma((groups, outer, inner)),
            dma((groups, outer, inner)),
            dma((CHUNKS, outer)),
            dma((groups, outer)),
        ],
        compiler_params=pltpu.CompilerParams(
            collective_id=0, has_side_effects=True, vmem_limit_bytes=60 * 1024 * 1024
        ),
        cost_estimate=pl.CostEstimate(
            flops=4 * block * basis * occupied, bytes_accessed=4 * block * basis, transcendentals=0
        ),
    )(integrals, coefficients, screen)


def solution(mesh):
    in_specs = (
        P(("parts", "aux"), "rows", None),
        P(("parts", "rows"), None),
        P(("parts", "aux"), "rows", None),
    )
    out_specs = P(("parts", "rows"), "aux")
    body = functools.partial(local, mesh.shape["rows"])
    return jax.shard_map(body, mesh=mesh, in_specs=in_specs, out_specs=out_specs, check_vma=False)
```

```python
import functools

import jax
import jax.numpy as jnp
from jax import lax
from jax.experimental import pallas as pl
from jax.experimental.pallas import tpu as pltpu
from jax.sharding import PartitionSpec as P

MESH = pl.DeviceIdType.MESH
CHUNKS = 2
HUB_C = True


def split_rows(n):
    inner = 1
    while inner * inner * 4 <= n:
        inner *= 2
    return n // inner, inner


def table(outer, rank, z):
    code = 0
    for place in range(outer):
        others = sorted((k for k in range(outer) if k != place), key=lambda k: (abs(k - place), k))
        code += others[rank] * outer**place
    power = 1
    bit = 1
    while bit < outer:
        power = power * (1 + (outer**bit - 1) * ((z // bit) % 2))
        bit *= 2
    return (code // power) % outer


def remote(src, dst, send, recv, rows, aux):
    return pltpu.make_async_remote_copy(
        src_ref=src,
        dst_ref=dst,
        send_sem=send,
        recv_sem=recv,
        device_id={"rows": rows, "aux": aux},
        device_id_type=MESH,
    )


def kernel(
    outer,
    inner,
    a_hbm,
    c_hbm,
    screen_hbm,
    out_hbm,
    a,
    screen,
    c_own,
    ct,
    acc,
    own,
    left,
    h,
    out,
    load_sem,
    store_sem,
    a_send,
    a_recv,
    cz_send,
    cz_recv,
    cy_send,
    cy_recv,
    hs_send,
    hs_recv,
    hz_send,
    hz_recv,
    hy_send,
    hy_recv,
    cf_send,
    ho_send,
    k_send,
    k_recv,
):
    n = outer * inner
    block, occupied = c_hbm.shape
    ho = outer // 2
    width = occupied // 2
    ic = width // CHUNKS
    groups = 2 * CHUNKS
    me = lax.axis_index("rows")
    core = lax.axis_index("aux")
    sib = 1 - core
    z = me // inner
    y = me % inner
    owner = z // ho

    mine_i = pl.ds(pl.multiple_of(core * width, width), width)
    load_c = pltpu.make_async_copy(c_hbm.at[:, mine_i], c_own, load_sem.at[1])
    load_a = pltpu.make_async_copy(a_hbm.at[0], a.at[core], load_sem.at[0])
    load_s = pltpu.make_async_copy(screen_hbm, screen, load_sem.at[2])
    load_c.start()
    load_s.start()
    load_a.start()

    zs = [table(outer, rank, z) for rank in range(outer - 1)]
    ys = [(y + k) % inner for k in range(1, inner)]
    hub = outer == 4
    hub_c = hub and HUB_C
    mate = z + 1 - 2 * (z % 2)
    inside = ((z + 1) // 2) % 2
    direct = [2 - z // 2, mate] if hub else zs[::-1]

    barrier = pltpu.get_barrier_semaphore()
    def greet(rows, aux):
        pl.semaphore_signal(
            barrier, inc=1, device_id={"rows": rows, "aux": aux}, device_id_type=MESH
        )

    for k in range(2):
        if hub_c:
            greet(mate * inner + y, k)
        else:
            for other in zs:
                greet(other * inner + y, k)
    if hub_c:

        @pl.when(inside == 1)
        def _():
            for k in range(2):
                for j in range(2):
                    greet((2 * (1 - z // 2) + j) * inner + y, k)

    for other in ys:
        greet(z * inner + other, core)
    greet(me, sib)

    load_c.wait()
    turned = c_own[...].T
    for q in range(CHUNKS):
        ct[q, me] = turned[q * ic : (q + 1) * ic]

    pl.semaphore_wait(barrier, 2 * (2 if hub_c else outer - 1) + inner)

    sends = []

    def start(copy):
        copy.start()
        sends.append(copy)

    def wait_recv(ref, sem):
        remote(ref, ref, a_send.at[0], sem, me, sib).wait_recv()

    def c_along_y(q, source):
        ref = ct.at[q, source * inner + y]
        for other in ys:
            start(
                remote(
                    ref,
                    ref,
                    cy_send.at[q, source, other],
                    cy_recv.at[q, source, y],
                    z * inner + other,
                    core,
                )
            )

    for q in range(CHUNKS):
        for other in direct if hub_c else zs[::-1]:
            ref = ct.at[q, me]
            start(remote(ref, ref, cz_send.at[q, other], cz_recv.at[q, z], other * inner + y, core))
        c_along_y(q, z)

    load_s.wait()
    load_a.wait()
    for s in range(n):
        columns = pl.ds(s * block, block)
        flag = screen[0, 0, s].astype(jnp.float32)
        a[core, :, columns] = (a[core, :, columns].astype(jnp.float32) * flag).astype(a.dtype)
    start(remote(a.at[core], a.at[core], a_send.at[0], a_recv.at[0], me, sib))

    def c_onward(q, source):
        ref = ct.at[q, source * inner + y]
        return remote(
            ref, ref, cf_send.at[q, source], cz_recv.at[q, source], mate * inner + y, core
        )

    def c_from_z(q):
        for source in zs:
            wait_recv(ct.at[q, source * inner + y], cz_recv.at[q, source])
            if hub_c:

                @pl.when((inside == 1) & (source != mate))
                def _(source=source):
                    c_onward(q, source).start()

            c_along_y(q, source)

    nt = (((1,), (1,)), ((), ()))

    def product(q, s, first=False):
        columns = pl.ds(pl.multiple_of(s * block, block), block)
        for aux in range(2):
            term = lax.dot_general(
                ct[q, s], a[aux, :, columns], nt, preferred_element_type=jnp.float32
            )
            if first:
                acc[q, aux] = term
            else:
                acc[q, aux] += term

    def finish(q):
        g = core * CHUNKS + q
        ref = own.at[y, g]
        for aux in range(2):
            own[y, g, aux] = acc[q, aux].astype(own.dtype)
        for other in direct:
            start(
                remote(
                    ref,
                    h.at[z % ho, g],
                    hz_send.at[q, other],
                    hz_recv.at[g, z],
                    other * inner + y,
                    owner,
                )
            )
        for other in ys:
            start(
                remote(ref, ref, hy_send.at[q, other], hy_recv.at[q, y], z * inner + other, core)
            )
        start(remote(ref, ref, hs_send.at[q, y], hs_recv.at[q, y], me, sib))

    c_from_z(0)
    wait_recv(a.at[sib], a_recv.at[0])
    product(0, me, True)
    for source in zs:
        product(0, source * inner + y)
    for q in range(CHUNKS):
        if q + 1 < CHUNKS:
            c_from_z(q + 1)
        for source in [z] + zs:
            for other in ys:
                s = source * inner + other
                wait_recv(ct.at[q, s], cy_recv.at[q, source, other])
                product(q, s)
        finish(q)
        if q + 1 < CHUNKS:
            product(q + 1, me, True)
            for source in zs:
                product(q + 1, source * inner + y)

    def onward(g, source):
        ref = h.at[source % ho, g]
        return remote(
            ref, ref, ho_send.at[g, source], hz_recv.at[g, source], mate * inner + y, core
        )

    order = [core * ho + j + owner * (1 - core) * (ho - 1 - 2 * j) for j in range(ho)]

    for q in range(CHUNKS):
        for other in ys:
            ref = own.at[other, core * CHUNKS + q]
            wait_recv(ref, hy_recv.at[q, other])
            start(remote(ref, ref, hs_send.at[q, other], hs_recv.at[q, other], me, sib))
        if hub:
            for source in order:

                @pl.when((source != z) & (inside == 1) & (source != mate))
                def _(source=source, q=q):
                    for k in range(2):
                        g = k * CHUNKS + q
                        wait_recv(h.at[source % ho, g], hz_recv.at[g, source])
                        onward(g, source).start()

    for yy in [y] + ys:
        for q in range(CHUNKS):
            wait_recv(own.at[yy, sib * CHUNKS + q], hs_recv.at[q, yy])
        for aux in range(2):
            left[yy, aux] = jnp.concatenate([own[yy, g, aux] for g in range(groups)], axis=0).T

    def columns(source, yy):
        at = (source % ho) * inner + yy
        return pl.ds(pl.multiple_of(at * block, block), block)

    def product_of(yy, right):
        total = 0.0
        for aux in range(2):
            whole = jnp.concatenate([right[g, aux] for g in range(groups)], axis=0)
            term = jnp.dot(left[yy, aux], whole, preferred_element_type=jnp.float32)
            total = total + term.astype(out.dtype).astype(jnp.float32)
        return total.astype(out.dtype)

    def theirs(source, other):
        at = out_hbm.at[:, columns(source, y)]
        return remote(
            out.at[source % ho, other],
            at,
            k_send.at[source % ho, other],
            k_recv.at[source % ho, y],
            z * inner + other,
            core,
        )

    def ours(source):
        return pltpu.make_async_copy(
            out.at[source % ho, y], out_hbm.at[:, columns(source, y)], store_sem.at[source % ho]
        )

    def emit(source, right):
        for other in ys:
            out[source % ho, other] = product_of(other, right)
            theirs(source, other).start()
        out[source % ho, y] = product_of(y, right)
        ours(source).start()

    @pl.when(owner == core)
    def _():
        emit(z, own.at[y])

    for source in order:

        @pl.when(source != z)
        def _(source=source):
            right = h.at[source % ho]
            skip = (inside == 1) & (source != mate) if hub else False

            @pl.when(jnp.logical_not(skip))
            def _():
                for g in range(groups):
                    wait_recv(right.at[g], hz_recv.at[g, source])

            emit(source, right)

    for copy in sends:
        copy.wait_send()
    if hub_c:
        for source in zs:

            @pl.when((inside == 1) & (source != mate))
            def _(source=source):
                for q in range(CHUNKS):
                    c_onward(q, source).wait_send()

    if hub:
        for source in order:

            @pl.when((source != z) & (inside == 1) & (source != mate))
            def _(source=source):
                for g in range(groups):
                    onward(g, source).wait_send()

    for source in order:
        ours(source).wait()
        for other in ys:
            theirs(source, other).wait_send()
            at = out_hbm.at[:, columns(source, other)]
            wait_recv(at, k_recv.at[source % ho, other])


def local(n, integrals, coefficients, screen):
    outer, inner = split_rows(n)
    block, occupied = coefficients.shape
    dma = pltpu.SemaphoreType.DMA
    basis = n * block
    groups = 2 * CHUNKS
    ic = occupied // groups
    return pl.pallas_call(
        functools.partial(kernel, outer, inner),
        out_shape=jax.ShapeDtypeStruct((block, basis // 2), jnp.bfloat16),
        in_specs=[pl.BlockSpec(memory_space=pltpu.HBM)] * 3,
        out_specs=pl.BlockSpec(memory_space=pl.ANY),
        scratch_shapes=[
            pltpu.VMEM((2, block, basis), jnp.bfloat16),
            pltpu.SMEM(screen.shape, jnp.int32),
            pltpu.VMEM((block, occupied // 2), jnp.bfloat16),
            pltpu.VMEM((CHUNKS, n, ic, block), jnp.bfloat16),
            pltpu.VMEM((CHUNKS, 2, ic, block), jnp.float32),
            pltpu.VMEM((inner, groups, 2, ic, block), jnp.bfloat16),
            pltpu.VMEM((inner, 2, block, occupied), jnp.bfloat16),
            pltpu.VMEM((outer // 2, groups, 2, ic, block), jnp.bfloat16),
            pltpu.VMEM((outer // 2, inner, block, block), jnp.bfloat16),
            dma((3,)),
            dma((outer // 2,)),
            dma((1,)),
            dma((1,)),
            dma((CHUNKS, outer)),
            dma((CHUNKS, outer)),
            dma((CHUNKS, outer, inner)),
            dma((CHUNKS, outer, inner)),
            dma((CHUNKS, inner)),
            dma((CHUNKS, inner)),
            dma((CHUNKS, outer)),
            dma((groups, outer)),
            dma((CHUNKS, inner)),
            dma((CHUNKS, inner)),
            dma((CHUNKS, outer)),
            dma((groups, outer)),
            dma((outer // 2, inner)),
            dma((outer // 2, inner)),
        ],
        compiler_params=pltpu.CompilerParams(
            collective_id=0, has_side_effects=True, vmem_limit_bytes=60 * 1024 * 1024
        ),
        cost_estimate=pl.CostEstimate(
            flops=4 * block * basis * occupied, bytes_accessed=4 * block * basis, transcendentals=0
        ),
    )(integrals, coefficients, screen)


def solution(mesh):
    in_specs = (
        P(("parts", "aux"), "rows", None),
        P(("parts", "rows"), None),
        P(("parts", "aux"), "rows", None),
    )
    out_specs = P(("parts", "rows"), "aux")
    body = functools.partial(local, mesh.shape["rows"])
    return jax.shard_map(body, mesh=mesh, in_specs=in_specs, out_specs=out_specs, check_vma=False)
```

```python
import functools

import jax
import jax.numpy as jnp
from jax import lax
from jax.experimental import pallas as pl
from jax.experimental.pallas import tpu as pltpu
from jax.sharding import PartitionSpec as P

MESH = pl.DeviceIdType.MESH
CHUNKS = 2
HUB_C = True


def split_rows(n):
    inner = 1
    while inner * inner * 4 <= n:
        inner *= 2
    return n // inner, inner


def table(outer, rank, z):
    code = 0
    for place in range(outer):
        others = sorted((k for k in range(outer) if k != place), key=lambda k: (abs(k - place), k))
        code += others[rank] * outer**place
    power = 1
    bit = 1
    while bit < outer:
        power = power * (1 + (outer**bit - 1) * ((z // bit) % 2))
        bit *= 2
    return (code // power) % outer


def remote(src, dst, send, recv, rows, aux):
    return pltpu.make_async_remote_copy(
        src_ref=src,
        dst_ref=dst,
        send_sem=send,
        recv_sem=recv,
        device_id={"rows": rows, "aux": aux},
        device_id_type=MESH,
    )


def kernel(
    outer,
    inner,
    a_hbm,
    c_hbm,
    screen_hbm,
    out_hbm,
    a,
    screen,
    c_own,
    ct,
    acc,
    own,
    left,
    h,
    out,
    load_sem,
    store_sem,
    a_send,
    a_recv,
    cz_send,
    cz_recv,
    cy_send,
    cy_recv,
    hs_send,
    hs_recv,
    hz_send,
    hz_recv,
    hy_send,
    hy_recv,
    cf_send,
    ho_send,
    k_send,
    k_recv,
):
    n = outer * inner
    block, occupied = c_hbm.shape
    ho = outer // 2
    width = occupied // 2
    ic = width // CHUNKS
    groups = 2 * CHUNKS
    me = lax.axis_index("rows")
    core = lax.axis_index("aux")
    sib = 1 - core
    z = me // inner
    y = me % inner
    owner = z // ho

    mine_i = pl.ds(pl.multiple_of(core * width, width), width)
    load_c = pltpu.make_async_copy(c_hbm.at[:, mine_i], c_own, load_sem.at[1])
    load_a = pltpu.make_async_copy(a_hbm.at[0], a.at[core], load_sem.at[0])
    load_s = pltpu.make_async_copy(screen_hbm, screen, load_sem.at[2])
    load_c.start()
    load_s.start()
    load_a.start()

    zs = [table(outer, rank, z) for rank in range(outer - 1)]
    ys = [(y + k) % inner for k in range(1, inner)]
    hub = outer == 4
    hub_c = hub and HUB_C
    mate = z + 1 - 2 * (z % 2)
    inside = ((z + 1) // 2) % 2
    far = 3 * (1 - z // 2)
    direct = [2 - z // 2, mate] if hub else zs[::-1]

    barrier = pltpu.get_barrier_semaphore()
    def greet(rows, aux):
        pl.semaphore_signal(
            barrier, inc=1, device_id={"rows": rows, "aux": aux}, device_id_type=MESH
        )

    for k in range(2):
        if hub_c:
            greet(mate * inner + y, k)
        else:
            for other in zs:
                greet(other * inner + y, k)
    if hub_c:

        @pl.when(inside == 1)
        def _():
            for k in range(2):
                for j in range(2):
                    greet((2 * (1 - z // 2) + j) * inner + y, k)

        @pl.when(inside == 0)
        def _():
            for k in range(2):
                greet((2 - z // 2) * inner + y, k)

    for other in ys:
        greet(z * inner + other, core)
    greet(me, sib)

    load_c.wait()
    turned = c_own[...].T
    for q in range(CHUNKS):
        ct[q, me] = turned[q * ic : (q + 1) * ic]

    greeters = 2 * (2 + inside) if hub_c else 2 * (outer - 1)
    pl.semaphore_wait(barrier, greeters + inner)

    sends = []

    def start(copy):
        copy.start()
        sends.append(copy)

    def wait_recv(ref, sem):
        remote(ref, ref, a_send.at[0], sem, me, sib).wait_recv()

    def c_along_y(q, source):
        ref = ct.at[q, source * inner + y]
        for other in ys:
            start(
                remote(
                    ref,
                    ref,
                    cy_send.at[q, source, other],
                    cy_recv.at[q, source, y],
                    z * inner + other,
                    core,
                )
            )

    def c_far(q):
        ref = ct.at[q, me]
        return remote(ref, ref, cz_send.at[q, far], cz_recv.at[q, z], far * inner + y, core)

    for q in range(CHUNKS):
        for other in direct if hub_c else zs[::-1]:
            ref = ct.at[q, me]
            start(remote(ref, ref, cz_send.at[q, other], cz_recv.at[q, z], other * inner + y, core))
        c_along_y(q, z)
        if hub_c:

            @pl.when(inside == 1)
            def _(q=q):
                c_far(q).start()

    load_s.wait()
    load_a.wait()
    for s in range(n):
        columns = pl.ds(s * block, block)
        flag = screen[0, 0, s].astype(jnp.float32)
        a[core, :, columns] = (a[core, :, columns].astype(jnp.float32) * flag).astype(a.dtype)
    start(remote(a.at[core], a.at[core], a_send.at[0], a_recv.at[0], me, sib))

    def c_onward(q, source):
        ref = ct.at[q, source * inner + y]
        return remote(
            ref, ref, cf_send.at[q, source], cz_recv.at[q, source], mate * inner + y, core
        )

    def c_from_z(q):
        for source in zs:
            wait_recv(ct.at[q, source * inner + y], cz_recv.at[q, source])
            if hub_c:

                @pl.when((inside == 1) & (source == far))
                def _(source=source):
                    c_onward(q, source).start()

            c_along_y(q, source)

    nt = (((1,), (1,)), ((), ()))

    def product(q, s, first=False):
        columns = pl.ds(pl.multiple_of(s * block, block), block)
        for aux in range(2):
            term = lax.dot_general(
                ct[q, s], a[aux, :, columns], nt, preferred_element_type=jnp.float32
            )
            if first:
                acc[q, aux] = term
            else:
                acc[q, aux] += term

    def h_far(q):
        g = core * CHUNKS + q
        return remote(
            own.at[y, g],
            h.at[z % ho, g],
            hz_send.at[q, far],
            hz_recv.at[g, z],
            far * inner + y,
            owner,
        )

    def finish(q):
        g = core * CHUNKS + q
        ref = own.at[y, g]
        for aux in range(2):
            own[y, g, aux] = acc[q, aux].astype(own.dtype)
        for other in direct:
            start(
                remote(
                    ref,
                    h.at[z % ho, g],
                    hz_send.at[q, other],
                    hz_recv.at[g, z],
                    other * inner + y,
                    owner,
                )
            )
        if hub:

            @pl.when(inside == 1)
            def _():
                h_far(q).start()

        for other in ys:
            start(
                remote(ref, ref, hy_send.at[q, other], hy_recv.at[q, y], z * inner + other, core)
            )
        start(remote(ref, ref, hs_send.at[q, y], hs_recv.at[q, y], me, sib))

    c_from_z(0)
    wait_recv(a.at[sib], a_recv.at[0])
    product(0, me, True)
    for source in zs:
        product(0, source * inner + y)
    for q in range(CHUNKS):
        if q + 1 < CHUNKS:
            c_from_z(q + 1)
        for source in [z] + zs:
            for other in ys:
                s = source * inner + other
                wait_recv(ct.at[q, s], cy_recv.at[q, source, other])
                product(q, s)
        finish(q)
        if q + 1 < CHUNKS:
            product(q + 1, me, True)
            for source in zs:
                product(q + 1, source * inner + y)

    def onward(g, source):
        ref = h.at[source % ho, g]
        return remote(
            ref, ref, ho_send.at[g, source], hz_recv.at[g, source], mate * inner + y, core
        )

    order = [core * ho + j + owner * (1 - core) * (ho - 1 - 2 * j) for j in range(ho)]

    for q in range(CHUNKS):
        for other in ys:
            ref = own.at[other, core * CHUNKS + q]
            wait_recv(ref, hy_recv.at[q, other])
            start(remote(ref, ref, hs_send.at[q, other], hs_recv.at[q, other], me, sib))
        if hub:
            for source in order:

                @pl.when((source != z) & (inside == 1) & (source == far))
                def _(source=source, q=q):
                    for k in range(2):
                        g = k * CHUNKS + q
                        wait_recv(h.at[source % ho, g], hz_recv.at[g, source])
                        onward(g, source).start()

    for yy in [y] + ys:
        for q in range(CHUNKS):
            wait_recv(own.at[yy, sib * CHUNKS + q], hs_recv.at[q, yy])
        for aux in range(2):
            left[yy, aux] = jnp.concatenate([own[yy, g, aux] for g in range(groups)], axis=0).T

    def columns(source, yy):
        at = (source % ho) * inner + yy
        return pl.ds(pl.multiple_of(at * block, block), block)

    def product_of(yy, right):
        total = 0.0
        for aux in range(2):
            whole = jnp.concatenate([right[g, aux] for g in range(groups)], axis=0)
            term = jnp.dot(left[yy, aux], whole, preferred_element_type=jnp.float32)
            total = total + term.astype(out.dtype).astype(jnp.float32)
        return total.astype(out.dtype)

    def theirs(source, other):
        at = out_hbm.at[:, columns(source, y)]
        return remote(
            out.at[source % ho, other],
            at,
            k_send.at[source % ho, other],
            k_recv.at[source % ho, y],
            z * inner + other,
            core,
        )

    def ours(source):
        return pltpu.make_async_copy(
            out.at[source % ho, y], out_hbm.at[:, columns(source, y)], store_sem.at[source % ho]
        )

    def emit(source, right):
        for other in ys:
            out[source % ho, other] = product_of(other, right)
            theirs(source, other).start()
        out[source % ho, y] = product_of(y, right)
        ours(source).start()

    @pl.when(owner == core)
    def _():
        emit(z, own.at[y])

    for source in order:

        @pl.when(source != z)
        def _(source=source):
            right = h.at[source % ho]
            skip = (inside == 1) & (source == far) if hub else False

            @pl.when(jnp.logical_not(skip))
            def _():
                for g in range(groups):
                    wait_recv(right.at[g], hz_recv.at[g, source])

            emit(source, right)

    for copy in sends:
        copy.wait_send()
    if hub:

        @pl.when(inside == 1)
        def _():
            for q in range(CHUNKS):
                c_far(q).wait_send()
                h_far(q).wait_send()

    if hub_c:
        for source in zs:

            @pl.when((inside == 1) & (source == far))
            def _(source=source):
                for q in range(CHUNKS):
                    c_onward(q, source).wait_send()

    if hub:
        for source in order:

            @pl.when((source != z) & (inside == 1) & (source == far))
            def _(source=source):
                for g in range(groups):
                    onward(g, source).wait_send()

    for source in order:
        ours(source).wait()
        for other in ys:
            theirs(source, other).wait_send()
            at = out_hbm.at[:, columns(source, other)]
            wait_recv(at, k_recv.at[source % ho, other])


def local(n, integrals, coefficients, screen):
    outer, inner = split_rows(n)
    block, occupied = coefficients.shape
    dma = pltpu.SemaphoreType.DMA
    basis = n * block
    groups = 2 * CHUNKS
    ic = occupied // groups
    return pl.pallas_call(
        functools.partial(kernel, outer, inner),
        out_shape=jax.ShapeDtypeStruct((block, basis // 2), jnp.bfloat16),
        in_specs=[pl.BlockSpec(memory_space=pltpu.HBM)] * 3,
        out_specs=pl.BlockSpec(memory_space=pl.ANY),
        scratch_shapes=[
            pltpu.VMEM((2, block, basis), jnp.bfloat16),
            pltpu.SMEM(screen.shape, jnp.int32),
            pltpu.VMEM((block, occupied // 2), jnp.bfloat16),
            pltpu.VMEM((CHUNKS, n, ic, block), jnp.bfloat16),
            pltpu.VMEM((CHUNKS, 2, ic, block), jnp.float32),
            pltpu.VMEM((inner, groups, 2, ic, block), jnp.bfloat16),
            pltpu.VMEM((inner, 2, block, occupied), jnp.bfloat16),
            pltpu.VMEM((outer // 2, groups, 2, ic, block), jnp.bfloat16),
            pltpu.VMEM((outer // 2, inner, block, block), jnp.bfloat16),
            dma((3,)),
            dma((outer // 2,)),
            dma((1,)),
            dma((1,)),
            dma((CHUNKS, outer)),
            dma((CHUNKS, outer)),
            dma((CHUNKS, outer, inner)),
            dma((CHUNKS, outer, inner)),
            dma((CHUNKS, inner)),
            dma((CHUNKS, inner)),
            dma((CHUNKS, outer)),
            dma((groups, outer)),
            dma((CHUNKS, inner)),
            dma((CHUNKS, inner)),
            dma((CHUNKS, outer)),
            dma((groups, outer)),
            dma((outer // 2, inner)),
            dma((outer // 2, inner)),
        ],
        compiler_params=pltpu.CompilerParams(
            collective_id=0, has_side_effects=True, vmem_limit_bytes=60 * 1024 * 1024
        ),
        cost_estimate=pl.CostEstimate(
            flops=4 * block * basis * occupied, bytes_accessed=4 * block * basis, transcendentals=0
        ),
    )(integrals, coefficients, screen)


def solution(mesh):
    in_specs = (
        P(("parts", "aux"), "rows", None),
        P(("parts", "rows"), None),
        P(("parts", "aux"), "rows", None),
    )
    out_specs = P(("parts", "rows"), "aux")
    body = functools.partial(local, mesh.shape["rows"])
    return jax.shard_map(body, mesh=mesh, in_specs=in_specs, out_specs=out_specs, check_vma=False)
```
